128 devices in a mesh: dp: 16 (over y_hi, x, core), tensor: 8 (over z, y_lo).
Axes of the slice: x: 4, y: 4 (y_hi: 2, y_lo: 2; y = y_hi * 2 + y_lo), z: 4, core: 2. Of those that a mesh axis runs over, the one named last changes fastest.
Arguments:
- learn_hidden: bfloat16 [768, 4096], P('dp', 'tensor'), may hold values from -360 to 360
- target_hidden: bfloat16 [768, 4096], P('dp', 'tensor'), may hold values from -360 to 360
- reward: bfloat16 [768], P('dp'), may hold values from -6 to 6
- learn_head: bfloat16 [4096, 128256], P(None, ('dp', 'tensor')), may hold values from -0.09375 to 0.09375
- target_head: bfloat16 [4096, 128256], P(None, ('dp', 'tensor')), may hold values from -0.09375 to 0.09375
- action: int32 [768], P('dp'), may hold values from 0 to 128255
- traj_len: int32 [32], P('dp'), may hold values from 1 to 24, 576 in all
- owner: int32 [32], P('dp'), may hold values from 0 to 15
Outputs:
- head_grad: bfloat16 [4096, 128256], P(None, ('dp', 'tensor'))
- hidden_grad: bfloat16 [768, 4096], P('dp', 'tensor')
- priority: float32 [16, 24], P('dp')
The draws below stay inside these ranges and needn't reach their ends.
All inputs are finite; a program needn't handle non-finite values. No bound on the sum of `traj_len` on one device may be relied on, other than what follows from the above.
Results may differ from the reference program's by a relative error of at most 0.005.
Values may be sent and summed in bfloat16 or wider, within the bound.
No kernel may reach another device: no remote copies, remote signals or barrier semaphores. Data moves between devices by JAX's collectives and lax.ppermute only.
A program may use at most 128 MiB of HBM per device.

```python
import math
import jax
import jax.numpy as jnp
import numpy as np
from jax import lax

D = 4096
V = 128256
LEN = 24
TRAJ = 32
TOKENS = 768
OWNERS = 16


def rough_rows(key, lowest, highest):
    rows_key, cells_key = jax.random.split(key)
    cells = jnp.clip(jax.random.normal(cells_key, (TOKENS, D), jnp.float32), -6.0, 6.0)
    spread = jax.random.uniform(rows_key, (TOKENS, 1), jnp.float32, math.log(lowest), math.log(highest))
    return (cells * jnp.exp(spread)).astype(jnp.bfloat16)


def draw_learn_hidden(key, part):
    key = jax.random.fold_in(key, 11)
    return rough_rows(key, 3.0, 3.0)


def draw_target_hidden(key, part):
    key = jax.random.fold_in(key, 23)
    return rough_rows(key, 3.0, 3.0)


def with_ends(array, rng, low, top_value):
    index_at = [jax.random.randint(jax.random.fold_in(rng, axis), (), 0, length) for axis, length in enumerate(array.shape)]
    longest = array.shape.index(max(array.shape))
    next_to = index_at[:longest] + [(index_at[longest] + 1) % array.shape[longest]] + index_at[longest + 1:]
    return array.at[tuple(index_at)].set(low).at[tuple(next_to)].set(top_value)


def block_levels(stream_key, dims, shards, smallest, high):
    def one(dim, shards_of):
        steps = jax.random.uniform(jax.random.fold_in(jax.random.fold_in(stream_key, 6), dim), (shards_of,), jnp.float32, smallest / len(shards), high / len(shards))
        return jnp.repeat(jnp.exp(steps), dims[dim] // shards_of).reshape((-1,) + (1,) * (len(dims) - dim - 1))

    gain = one(*shards[0])
    for cut in shards[1:]:
        gain = gain * one(*cut)
    return gain


def wide_ids(rng, dims, number_of, lean):
    portions = [min(1 << octave, number_of + 1 - (1 << octave)) * (1 << 20) // math.isqrt((1 << octave) ** lean) + 1 for octave in range((number_of + 1).bit_length()) if 1 << octave <= number_of]
    scale = 1 + sum(portions) // (1 << 30)
    table = np.cumsum(np.array([max(1, weight // scale) for weight in portions]))
    ticket = jax.random.randint(jax.random.fold_in(rng, 1), dims, 0, int(table[len(portions) - 1]))
    start = jnp.left_shift(1, jnp.searchsorted(jnp.asarray(table, jnp.int32), ticket, side="right").astype(jnp.int32))
    standing = start - 1 + jax.random.randint(jax.random.fold_in(rng, 4), dims, 0, 1 << 30) % jnp.minimum(start, number_of + 1 - start)
    return jax.random.permutation(jax.random.fold_in(rng, 2), number_of)[standing].astype(jnp.int32)


def split_up(number_of, total, most, lean):
    weights = [(1 << 20) // math.isqrt(standing ** lean) + 1 for standing in range(2, number_of + 1)]
    rest, counts = total - most - (number_of - 1), [1] * (number_of - 1)
    while rest > 0:
        movable = [i for i in range(number_of - 1) if counts[i] < most]
        pool, remaining = sum([weights[i] for i in movable]), rest
        for i in movable:
            extra = min(most - counts[i], max(1, remaining * weights[i] // pool), rest)
            counts[i] = counts[i] + extra
            rest = rest - extra
    return np.array([most] + counts)


def ragged(stream_key, amount, total, most, skew):
    if amount == 2:
        one = jax.random.randint(stream_key, (), max(1, total - most), min(most, total - 1) + 1)
        return jnp.stack([one, total - one])
    tallies = jnp.asarray(split_up(amount, total, most, skew), jnp.int32)
    pairs = (amount - 1) // 2
    giver, receiver = tallies[1:1 + 2 * pairs:2], tallies[2:2 + 2 * pairs:2]
    margin = jnp.minimum(giver - 1, most - receiver)
    moved = jax.random.randint(jax.random.fold_in(stream_key, 1), (pairs,), 0, 1 << 20) % (margin + 1)
    tallies = tallies.at[1:1 + 2 * pairs:2].set(giver - moved).at[2:2 + 2 * pairs:2].set(receiver + moved)
    return tallies[jax.random.permutation(jax.random.fold_in(stream_key, 2), amount)]


def centred(stream_key, dims, deviation, most, cuts=(), kind=jnp.bfloat16):
    loudness = block_levels(stream_key, dims, cuts, -0.22, 0.18) if cuts else 1.0
    values = jax.random.normal(stream_key, dims, jnp.float32) * deviation * loudness
    return jnp.minimum(jnp.maximum(values, -most), most).astype(kind)


def setup_inputs(seed: int = 0) -> dict:
    keys = jax.random.split(jax.random.key(seed), 9)
    return {
        "learn_hidden": draw_learn_hidden(jax.random.fold_in(keys[8], 71), 0),
        "target_hidden": draw_target_hidden(jax.random.fold_in(keys[8], 71), 0),
        "reward": centred(keys[2], (TOKENS,), 1.0, 6.0, ((0, 16),)),
        "learn_head": centred(keys[3], (D, V), D ** -0.5, 0.09375, ((1, 128),)),
        "target_head": centred(keys[4], (D, V), D ** -0.5, 0.09375, ((1, 128),)),
        "action": with_ends(wide_ids(keys[5], (TOKENS,), V, 2), jax.random.fold_in(keys[5], 3), 0, V - 1).astype(jnp.int32),
        "traj_len": ragged(keys[6], TRAJ, TRAJ * LEN * 3 // 4, LEN, 2).astype(jnp.int32),
        "owner": with_ends(jax.random.randint(keys[7], (TRAJ,), 0, OWNERS), jax.random.fold_in(keys[7], 1), 0, OWNERS - 1).astype(jnp.int32),
    }


temper = 1.0
discount = 0.99
kl_weight = 10.0


def soft_stats(logits):
    row_max = jnp.max(logits, axis=1, keepdims=True)
    expo = jnp.exp((logits - row_max) / temper)
    total = jnp.sum(expo, axis=1, keepdims=True)
    value = row_max[:, 0] + temper * jnp.log(total[:, 0])
    return value, expo / total


def reference(learn_hidden, target_hidden, reward, learn_head, target_head, action, traj_len, owner):
    learn_q = jnp.dot(learn_hidden, learn_head, preferred_element_type=jnp.float32)
    target_q = jnp.dot(target_hidden, target_head, preferred_element_type=jnp.float32)
    learn_value, learn_p = soft_stats(learn_q)
    target_value, target_p = soft_stats(target_q)
    position = jnp.arange(TOKENS, dtype=jnp.int32)
    offset = position % LEN
    lengths = jnp.repeat(traj_len, LEN)
    live = (offset < lengths).astype(jnp.float32)
    follow = (offset + 1 < lengths).astype(jnp.float32)
    hits = action[:, None] == jnp.arange(V, dtype=jnp.int32)[None, :]
    picked = jnp.sum(jnp.where(hits, learn_q, 0.0), axis=1)
    shifted = jnp.concatenate([target_value[1:], jnp.zeros((1,), jnp.float32)])
    target_y = reward.astype(jnp.float32) + discount * follow * shifted
    delta = live * (picked - target_y)
    grad_q = (jnp.where(hits, delta[:, None], 0.0) + kl_weight * live[:, None] * (learn_p - target_p) / temper) / TRAJ
    grad_q = grad_q.astype(jnp.bfloat16)
    head_grad = lax.dot_general(learn_hidden, grad_q, (((0,), (0,)), ((), ())), preferred_element_type=jnp.float32).astype(jnp.bfloat16)
    hidden_grad = lax.dot_general(grad_q, learn_head, (((1,), (1,)), ((), ())), preferred_element_type=jnp.float32).astype(jnp.bfloat16)
    owner_table = (jnp.arange(OWNERS, dtype=jnp.int32)[:, None] == owner[None, :]).astype(jnp.float32)
    priority = jnp.dot(owner_table, jnp.abs(delta).reshape(TRAJ, LEN), precision=lax.Precision.HIGHEST)
    return head_grad, hidden_grad, priority
```

```python
import functools

import jax
import jax.numpy as jnp
from jax import lax
from jax.experimental import pallas as pl
from jax.experimental.pallas import tpu as pltpu
from jax.sharding import Mesh, PartitionSpec as P

temper = 1.0
discount = 0.99
kl_weight = 10.0

DP = ("yh", "x", "c")
TENSOR = ("z", "yl")
PLANE = ("yh", "x", "z", "yl")
Y = ("yh", "yl")


def shift(v, axis, by):
    return lax.ppermute(v, axis, [(i, (i + by) % 4) for i in range(4)])


def swap_cores(v):
    return lax.ppermute(v, "c", [(0, 1), (1, 0)])


def gather_ring(v, axis):
    me = lax.axis_index(axis)
    arrived = [v] + [shift(v, axis, by) for by in (1, 3, 2)]
    out = jnp.zeros((4,) + v.shape, v.dtype)
    for by, block in zip((0, 1, 3, 2), arrived):
        out = lax.dynamic_update_index_in_dim(out, block, (me - by) & 3, 0)
    return out


VMEM_LIMIT = 40 * 1024 * 1024
NT = (((1,), (1,)), ((), ()))
NN = (((1,), (0,)), ((), ()))


def whole(shape):
    return pl.BlockSpec(shape, lambda j: (0,) * len(shape))


def hidden_spec(shape, x_first):
    rows, feats = shape[-2:]
    if x_first:
        return pl.BlockSpec((4, 2, 1, 1, rows, feats), lambda j: (0, 0, j % 2, j // 2, 0, 0))
    return pl.BlockSpec((2, 1, 4, 1, rows, feats), lambda j: (0, j % 2, 0, j // 2, 0, 0))


def hidden_block(ref, x_first):
    rows, feats = ref.shape[-2:]
    if x_first:
        return jnp.concatenate([ref[x, yh, 0, 0] for yh in range(2) for x in range(4)], axis=0)
    return ref[...].reshape(8 * rows, feats)


def cost(flops, nbytes, exps=0):
    return pl.CostEstimate(flops=flops, bytes_accessed=nbytes, transcendentals=exps)


def q_kernel(x_first, row, base_ref, action_ref, hidden_ref, own_ref, sib_ref, q_own, q_sib, stats_ref):
    j = pl.program_id(0)
    hidden = hidden_block(hidden_ref, x_first)
    for head_ref, q_ref in ((own_ref, q_own), (sib_ref, q_sib)):
        part = lax.dot_general(head_ref[...], hidden, NT, preferred_element_type=jnp.float32)

        @pl.when(j == 0)
        def _():
            q_ref[...] = part

        @pl.when(j > 0)
        def _():
            q_ref[...] += part

    @pl.when(j == pl.num_programs(0) - 1)
    def _():
        peak = jnp.maximum(
            jnp.max(q_own[...], axis=0, keepdims=True), jnp.max(q_sib[...], axis=0, keepdims=True)
        )
        total = jnp.zeros_like(peak)
        picked = jnp.zeros_like(peak)
        ids = lax.broadcasted_iota(jnp.int32, q_own.shape, 0)
        for k, q_ref in enumerate((q_own, q_sib)):
            q = q_ref[...]
            total += jnp.sum(jnp.exp((q - peak) / temper), axis=0, keepdims=True)
            if row == 0:
                hit = ids == action_ref[...] - base_ref[k]
                picked += jnp.sum(jnp.where(hit, q, 0.0), axis=0, keepdims=True)
        stats_ref[...] = jnp.zeros_like(stats_ref)
        stats_ref[row : row + 1] = peak
        stats_ref[row + 1 : row + 2] = total
        if row == 0:
            stats_ref[4:5] = picked


def q_values(hidden, heads, bases, action, x_first, row):
    width, feats_all = heads[0].shape
    feats = hidden.shape[-1]
    tokens = action.shape[1]
    steps = feats_all // feats
    head_spec = pl.BlockSpec((width, feats), lambda j: (0, j))
    q_shape = jax.ShapeDtypeStruct((width, tokens), jnp.float32)
    return pl.pallas_call(
        functools.partial(q_kernel, x_first, row),
        grid=(steps,),
        in_specs=[
            pl.BlockSpec(memory_space=pltpu.SMEM),
            whole(action.shape),
            hidden_spec(hidden.shape, x_first),
            head_spec,
            head_spec,
        ],
        out_specs=[whole(q_shape.shape)] * 2 + [whole((8, tokens))],
        out_shape=[q_shape, q_shape, jax.ShapeDtypeStruct((8, tokens), jnp.float32)],
        compiler_params=pltpu.CompilerParams(vmem_limit_bytes=VMEM_LIMIT),
        cost_estimate=cost(
            4 * tokens * width * feats_all, 4 * width * feats_all + 2 * tokens * feats_all, 2 * tokens * width
        ),
    )(bases, action, hidden, *heads)


def grad_kernel(
    scale, base_ref, action_ref, vec_ref, lq_own, lq_sib, tq_own, tq_sib, own_ref, sib_ref,
    grad_own, grad_sib, part_ref, g_own, g_sib,
):
    @pl.when(pl.program_id(0) == 0)
    def _():
        learn_max, learn_gain, target_max, target_gain, delta = (vec_ref[k : k + 1] for k in range(5))
        ids = lax.broadcasted_iota(jnp.int32, lq_own.shape, 0)
        for k, (lq, tq, out, flat) in enumerate(
            ((lq_own, tq_own, grad_own, g_own), (lq_sib, tq_sib, grad_sib, g_sib))
        ):
            learn_p = jnp.exp((lq[...] - learn_max) / temper) * learn_gain
            target_p = jnp.exp((tq[...] - target_max) / temper) * target_gain
            hit = ids == action_ref[...] - base_ref[k]
            grad = (jnp.where(hit, delta, 0.0) + (learn_p - target_p) / temper) * scale
            out[...] = grad.astype(jnp.bfloat16)
            flat[...] = grad.T.astype(jnp.bfloat16)

    part = lax.dot_general(g_own[...], own_ref[...], NN, preferred_element_type=jnp.float32)
    part += lax.dot_general(g_sib[...], sib_ref[...], NN, preferred_element_type=jnp.float32)
    part_ref[...] = part.astype(jnp.bfloat16).reshape(part_ref.shape)


def gradients(lq, tq, heads, bases, action, vec, rows, feats, traj_total):
    width, feats_all = heads[0].shape
    tokens = action.shape[1]
    steps = feats_all // feats
    head_spec = pl.BlockSpec((width, feats), lambda j: (0, j))
    g_shape = jax.ShapeDtypeStruct((width, tokens), jnp.bfloat16)
    return pl.pallas_call(
        functools.partial(grad_kernel, 1.0 / traj_total),
        grid=(steps,),
        in_specs=[pl.BlockSpec(memory_space=pltpu.SMEM), whole(action.shape), whole(vec.shape)]
        + [whole((width, tokens))] * 4
        + [head_spec] * 2,
        out_specs=[whole((width, tokens))] * 2
        + [pl.BlockSpec((tokens // rows, 1, rows, feats), lambda j: (0, j, 0, 0))],
        out_shape=[g_shape, g_shape]
        + [jax.ShapeDtypeStruct((tokens // rows, steps, rows, feats), jnp.bfloat16)],
        scratch_shapes=[pltpu.VMEM((tokens, width), jnp.bfloat16)] * 2,
        compiler_params=pltpu.CompilerParams(vmem_limit_bytes=VMEM_LIMIT),
        cost_estimate=cost(
            4 * tokens * width * feats_all, 4 * width * feats_all + 2 * tokens * feats_all, 4 * tokens * width
        ),
    )(bases, action, vec, *lq, *tq, *heads)


def head_kernel(x_first, grad_ref, hidden_ref, *refs):
    out_ref = refs[-1]
    total = lax.dot_general(
        grad_ref[...], hidden_block(hidden_ref, x_first), NN, preferred_element_type=jnp.float32
    )
    if len(refs) > 1:
        total += refs[0][...].astype(jnp.float32)
    out_ref[...] = total.astype(jnp.bfloat16)


def head_part(grad, hidden, x_first, *more):
    width, tokens = grad.shape
    feats = hidden.shape[-1]
    steps = 8
    spec = pl.BlockSpec((width, feats), lambda j: (0, j))
    return pl.pallas_call(
        functools.partial(head_kernel, x_first),
        grid=(steps,),
        in_specs=[whole(grad.shape), hidden_spec(hidden.shape, x_first)] + [spec] * len(more),
        out_specs=spec,
        out_shape=jax.ShapeDtypeStruct((width, steps * feats), jnp.bfloat16),
        compiler_params=pltpu.CompilerParams(vmem_limit_bytes=VMEM_LIMIT),
        cost_estimate=cost(
            2 * tokens * width * steps * feats, (2 * width + 2 * tokens + 2 * width * len(more)) * steps * feats
        ),
    )(grad, hidden, *more)


def shards(learn_hidden, target_hidden, reward, learn_head, target_head, action, traj_len, owner):
    f32, bf16 = jnp.float32, jnp.bfloat16
    rows, feats = learn_hidden.shape
    width = learn_head.shape[1]
    trajs = traj_len.shape[0]
    tokens = rows * 8
    seq_len = rows // trajs
    traj_total = trajs * 16

    learn_head, target_head = learn_head.T, target_head.T
    learn_sib, target_sib = swap_cores(learn_head), swap_cores(target_head)

    small = jnp.concatenate(
        [action.astype(f32), reward.astype(f32), traj_len.astype(f32), owner.astype(f32)]
    )
    small = jnp.pad(small, (0, 128 - small.shape[0]))

    both = gather_ring(jnp.stack([learn_hidden, target_hidden]), "z")
    learn = gather_ring(both[:, 0], "x")
    target = gather_ring(both[:, 1], Y)
    learn, target, learn_sib, target_sib, small = lax.optimization_barrier(
        (learn, target, learn_sib, target_sib, small)
    )
    learn = gather_ring(learn, Y).reshape(2, 2, 4, 4, rows, feats)
    target = gather_ring(target, "x").reshape(4, 2, 2, 4, rows, feats)
    learn_heads, target_heads = (learn_head, learn_sib), (target_head, target_sib)

    small = lax.all_to_all(
        jnp.broadcast_to(small[None, None], (8, 8, 128)), ("yh", "x"), 0, 0, tiled=True
    )[:, 0]
    action_all = small[:, :rows].reshape(1, tokens).astype(jnp.int32)
    reward_all = small[:, rows : 2 * rows].reshape(tokens)
    length_all = small[:, 2 * rows : 2 * rows + trajs].reshape(8 * trajs).astype(jnp.int32)
    owner_all = small[:, 2 * rows + trajs : 2 * rows + 2 * trajs].reshape(8 * trajs).astype(jnp.int32)

    core = lax.axis_index("c")
    dp = lax.axis_index(DP)
    tensor = lax.axis_index(TENSOR)
    bases = jnp.stack([((dp + (1 - 2 * core) * k) * 8 + tensor) * width for k in (0, 1)])

    *learn_q, learn_stats = q_values(learn, learn_heads, bases, action_all, False, 0)
    *target_q, target_stats = q_values(target, target_heads, bases, action_all, True, 2)

    packed = learn_stats + target_stats
    packed = lax.all_to_all(
        jnp.broadcast_to(packed[None], (64,) + packed.shape), PLANE, 0, 0, tiled=True
    )
    learn_max = jnp.max(packed[:, 0], axis=0)
    target_max = jnp.max(packed[:, 2], axis=0)
    learn_sum = jnp.sum(packed[:, 1] * jnp.exp((packed[:, 0] - learn_max) / temper), axis=0)
    target_sum = jnp.sum(packed[:, 3] * jnp.exp((packed[:, 2] - target_max) / temper), axis=0)
    picked = jnp.sum(packed[:, 4], axis=0)

    target_value = target_max + temper * jnp.log(target_sum)
    offset = jnp.arange(tokens, dtype=jnp.int32) % seq_len
    lengths = jnp.repeat(length_all, seq_len)
    live = (offset < lengths).astype(f32)
    follow = (offset + 1 < lengths).astype(f32)
    shifted = jnp.concatenate([target_value[1:], jnp.zeros((1,), f32)])
    target_y = reward_all + discount * follow * shifted
    delta = live * (picked - target_y)

    zero = jnp.zeros_like(delta)
    vec = jnp.stack(
        [
            learn_max,
            kl_weight * live / learn_sum,
            target_max,
            kl_weight * live / target_sum,
            delta,
            zero,
            zero,
            zero,
        ]
    )
    grad_own, grad_sib, partial = gradients(
        learn_q, target_q, learn_heads, bases, action_all, vec, rows, feats, traj_total
    )

    partial = lax.all_to_all(partial.reshape(64, rows, feats), PLANE, 0, 0, tiled=True)
    hidden_grad = jnp.sum(partial.astype(f32), axis=0).astype(bf16)

    theirs = swap_cores(head_part(grad_sib, learn, False))
    head_grad = head_part(grad_own, learn, False, theirs).T

    magnitude = jnp.abs(delta).reshape(8 * trajs, seq_len)
    owner_table = (jnp.arange(16, dtype=jnp.int32)[:, None] == owner_all[None, :]).astype(f32)
    sums = jnp.dot(owner_table, magnitude, precision=lax.Precision.HIGHEST)
    sums = sums + swap_cores(sums)
    priority = lax.dynamic_slice_in_dim(sums, dp, 1, 0)
    return (head_grad, hidden_grad, priority)


def solution(mesh):
    fine = Mesh(mesh.devices.reshape(2, 4, 2, 4, 2), ("yh", "x", "c", "z", "yl"))
    vocab = P(None, DP + TENSOR)
    return jax.shard_map(
        shards,
        mesh=fine,
        in_specs=(P(DP, TENSOR), P(DP, TENSOR), P(DP), vocab, vocab, P(DP), P(DP), P(DP)),
        out_specs=(vocab, P(DP, TENSOR), P(DP, None)),
        check_vma=False,
    )
```

```python
import functools

import jax
import jax.numpy as jnp
from jax import lax
from jax.experimental import pallas as pl
from jax.experimental.pallas import tpu as pltpu
from jax.sharding import Mesh, PartitionSpec as P

temper = 1.0
discount = 0.99
kl_weight = 10.0

DP = ("yh", "x", "c")
TENSOR = ("z", "yl")
PLANE = ("yh", "x", "z", "yl")
Y = ("yh", "yl")


def shift(v, axis, by):
    return lax.ppermute(v, axis, [(i, (i + by) % 4) for i in range(4)])


def swap_cores(v):
    return lax.ppermute(v, "c", [(0, 1), (1, 0)])


def ring_blocks(v, axis):
    ahead, back, across = (shift(v, axis, by) for by in (1, 3, 2))
    return v, ahead, across, back


def gather_ring(v, axis):
    me = lax.axis_index(axis)
    out = jnp.zeros((4,) + v.shape, v.dtype)
    for by, block in enumerate(ring_blocks(v, axis)):
        out = lax.dynamic_update_index_in_dim(out, block, (me - by) & 3, 0)
    return out


VMEM_LIMIT = 60 * 1024 * 1024
NT = (((1,), (1,)), ((), ()))
NN = (((1,), (0,)), ((), ()))


def whole(shape):
    return pl.BlockSpec(shape, lambda j: (0,) * len(shape))


def cost(flops, nbytes, exps=0):
    return pl.CostEstimate(flops=flops, bytes_accessed=nbytes, transcendentals=exps)


def columns_of(ref):
    turned = jnp.concatenate([ref[...]] * 16, axis=0).T
    return [turned[:, k : k + 1] for k in range(8)]


def place_blocks(x_ring, ids_ref, blocks, out_ref):
    rows, feats = blocks[0].shape[-2:]
    for by, block in enumerate(blocks):
        place = (ids_ref[2] - by) & 3
        if x_ring:
            for y in range(4):
                at = pl.multiple_of(((y // 2) * 4 + place) * rows, rows)
                out_ref[pl.ds(at, rows), (y % 2) * feats : (y % 2 + 1) * feats] = block[y]
        else:
            at = pl.multiple_of((place // 2) * 4 * rows, 4 * rows)
            lane = pl.multiple_of((place % 2) * feats, feats)
            out_ref[pl.ds(at, 4 * rows), pl.ds(lane, feats)] = block[...].reshape(4 * rows, feats)


def q_kernel(x_ring, ids_ref, vec_ref, b0, b1, b2, b3, own_ref, sib_ref, e_own, e_sib, stats_ref, hidden_ref):
    j = pl.program_id(0)
    place_blocks(x_ring, ids_ref, (b0, b1, b2, b3), hidden_ref)
    for head_ref, q_ref in ((own_ref, e_own), (sib_ref, e_sib)):
        part = lax.dot_general(hidden_ref[...], head_ref[...], NT, preferred_element_type=jnp.float32)

        @pl.when(j == 0)
        def _():
            q_ref[...] = part

        @pl.when(j > 0)
        def _():
            q_ref[...] += part

    @pl.when(j == pl.num_programs(0) - 1)
    def _():
        peak = jnp.maximum(
            jnp.max(e_own[...], axis=1, keepdims=True), jnp.max(e_sib[...], axis=1, keepdims=True)
        )
        total = jnp.zeros_like(peak)
        picked = jnp.zeros_like(peak)
        if not x_ring:
            action = columns_of(vec_ref)[0].astype(jnp.int32)
            ids = lax.broadcasted_iota(jnp.int32, e_own.shape, 1)
        for k, q_ref in enumerate((e_own, e_sib)):
            q = q_ref[...]
            if not x_ring:
                hit = ids == action - ids_ref[k]
                picked += jnp.sum(jnp.where(hit, q, 0.0), axis=1, keepdims=True)
            expo = jnp.exp((q - peak) / temper)
            total += jnp.sum(expo, axis=1, keepdims=True)
            q_ref[...] = expo
        lane = lax.broadcasted_iota(jnp.int32, (peak.shape[0], 128), 1)
        first = 2 if x_ring else 0
        table = jnp.where(lane == first, peak, jnp.where(lane == first + 1, total, 0.0))
        if not x_ring:
            table = jnp.where(lane == 4, picked, table)
        stats_ref[...] = table.T[:8]


def q_values(blocks, heads, ids, vec, x_ring, rows):
    width, feats_all = heads[0].shape
    feats = blocks[0].shape[-1]
    tokens = vec.shape[1]
    block_spec = pl.BlockSpec((4, rows, feats), lambda j: (0, j, 0))
    head_spec = pl.BlockSpec((width, 2 * feats), lambda j: (0, j))
    hidden_spec = pl.BlockSpec((tokens, 2 * feats), lambda j: (0, j))
    q_shape = jax.ShapeDtypeStruct((tokens, width), jnp.float32)
    stats_shape = jax.ShapeDtypeStruct((8, tokens), jnp.float32)
    hidden_shape = jax.ShapeDtypeStruct((tokens, feats_all), jnp.bfloat16)
    outs = [q_shape, q_shape, stats_shape]
    out_specs = [whole(o.shape) for o in outs]
    scratch = [pltpu.VMEM((tokens, 2 * feats), jnp.bfloat16)]
    if not x_ring:
        outs, out_specs, scratch = outs + [hidden_shape], out_specs + [hidden_spec], []
    return pl.pallas_call(
        functools.partial(q_kernel, x_ring),
        grid=(feats_all // (2 * feats),),
        in_specs=[pl.BlockSpec(memory_space=pltpu.SMEM), whole(vec.shape)] + [block_spec] * 4 + [head_spec] * 2,
        out_specs=out_specs,
        out_shape=outs,
        scratch_shapes=scratch,
        compiler_params=pltpu.CompilerParams(vmem_limit_bytes=VMEM_LIMIT),
        cost_estimate=cost(
            4 * tokens * width * feats_all, 4 * width * feats_all + 2 * tokens * feats_all, 2 * tokens * width
        ),
    )(ids, vec, *blocks, *heads)


def grad_kernel(
    scale, ids_ref, vec_ref, le_own, le_sib, te_own, te_sib, own_ref, sib_ref,
    turned_own, turned_sib, part_ref, g_own, g_sib,
):
    @pl.when(pl.program_id(0) == 0)
    def _():
        action, learn_gain, target_gain, delta = columns_of(vec_ref)[:4]
        action = action.astype(jnp.int32)
        ids = lax.broadcasted_iota(jnp.int32, le_own.shape, 1)
        for k, (le, te, out, turned) in enumerate(
            ((le_own, te_own, g_own, turned_own), (le_sib, te_sib, g_sib, turned_sib))
        ):
            hit = ids == action - ids_ref[k]
            both = le[...] * learn_gain - te[...] * target_gain
            grad = (jnp.where(hit, delta, 0.0) + both / temper) * scale
            out[...] = grad.astype(jnp.bfloat16)
            turned[...] = grad.T.astype(jnp.bfloat16)

    part = lax.dot_general(g_own[...], own_ref[...], NN, preferred_element_type=jnp.float32)
    part += lax.dot_general(g_sib[...], sib_ref[...], NN, preferred_element_type=jnp.float32)
    part = part.astype(jnp.bfloat16)
    groups, _, rows, feats = part_ref.shape
    for k in range(2):
        part_ref[:, k] = part[:, k * feats : (k + 1) * feats].reshape(groups, rows, feats)


def gradients(learn_e, target_e, heads, ids, vec, rows, feats, traj_total):
    width, feats_all = heads[0].shape
    tokens = vec.shape[1]
    groups = tokens // rows
    head_spec = pl.BlockSpec((width, 2 * feats), lambda j: (0, j))
    g_shape = jax.ShapeDtypeStruct((width, tokens), jnp.bfloat16)
    return pl.pallas_call(
        functools.partial(grad_kernel, 1.0 / traj_total),
        grid=(feats_all // (2 * feats),),
        in_specs=[pl.BlockSpec(memory_space=pltpu.SMEM), whole(vec.shape)]
        + [whole((tokens, width))] * 4
        + [head_spec] * 2,
        out_specs=[whole((width, tokens))] * 2
        + [pl.BlockSpec((groups, 2, rows, feats), lambda j: (0, j, 0, 0))],
        out_shape=[g_shape, g_shape]
        + [jax.ShapeDtypeStruct((groups, feats_all // feats, rows, feats), jnp.bfloat16)],
        scratch_shapes=[pltpu.VMEM((tokens, width), jnp.bfloat16)] * 2,
        compiler_params=pltpu.CompilerParams(vmem_limit_bytes=VMEM_LIMIT),
        cost_estimate=cost(
            4 * tokens * width * feats_all, 4 * width * feats_all + 2 * tokens * feats_all, 0
        ),
    )(ids, vec, *learn_e, *target_e, *heads)


def head_kernel(grad_a, grad_b, hidden_a, hidden_b, out_ref):
    total = lax.dot_general(grad_a[...], hidden_a[...], NN, preferred_element_type=jnp.float32)
    total += lax.dot_general(grad_b[...], hidden_b[...], NN, preferred_element_type=jnp.float32)
    out_ref[...] = total.astype(jnp.bfloat16)


def head_gradient(grads, hiddens):
    width, tokens = grads[0].shape
    feats_all = hiddens[0].shape[1]
    block = feats_all // 4
    return pl.pallas_call(
        head_kernel,
        grid=(4,),
        in_specs=[whole((width, tokens))] * 2 + [pl.BlockSpec((tokens, block), lambda j: (0, j))] * 2,
        out_specs=pl.BlockSpec((width, block), lambda j: (0, j)),
        out_shape=jax.ShapeDtypeStruct((width, feats_all), jnp.bfloat16),
        compiler_params=pltpu.CompilerParams(vmem_limit_bytes=VMEM_LIMIT),
        cost_estimate=cost(4 * tokens * width * feats_all, (2 * width + 4 * tokens) * feats_all),
    )(*grads, *hiddens)


def shards(learn_hidden, target_hidden, reward, learn_head, target_head, action, traj_len, owner):
    f32, bf16 = jnp.float32, jnp.bfloat16
    rows, feats = learn_hidden.shape
    width = learn_head.shape[1]
    trajs = traj_len.shape[0]
    tokens = rows * 8
    seq_len = rows // trajs
    traj_total = trajs * 16

    learn_head, target_head = learn_head.T, target_head.T
    learn_sib, target_sib = swap_cores(learn_head), swap_cores(target_head)

    extra = [action & 255, (action >> 8) & 255, action >> 16, reward, traj_len, owner]
    extra = jnp.concatenate([v.astype(bf16) for v in extra])
    extra = jnp.pad(extra[None], ((0, 15), (0, feats - extra.shape[0])))

    both = gather_ring(jnp.stack([learn_hidden, target_hidden]), "z")
    learn = gather_ring(jnp.concatenate([both[:, 0].reshape(4 * rows, feats), extra]), "x")
    target = gather_ring(both[:, 1], Y)
    learn, target, learn_sib, target_sib = lax.optimization_barrier(
        (learn, target, learn_sib, target_sib)
    )
    learn_blocks = ring_blocks(learn, Y)
    target_blocks = ring_blocks(target.reshape(4, 4 * rows, feats), "x")
    learn_heads, target_heads = (learn_head, learn_sib), (target_head, target_sib)

    mine, other = (learn_blocks[by][:, 4 * rows].astype(f32) for by in (0, 2))
    lower = lax.axis_index("yh") == 0
    small = jnp.concatenate([jnp.where(lower, mine, other), jnp.where(lower, other, mine)])

    def field(at, size):
        return small[:, at : at + size].reshape(8 * size)

    action_all = field(0, rows) + 256.0 * field(rows, rows) + 65536.0 * field(2 * rows, rows)
    reward_all = field(3 * rows, rows)
    length_all = field(4 * rows, trajs).astype(jnp.int32)
    owner_all = field(4 * rows + trajs, trajs).astype(jnp.int32)

    core = lax.axis_index("c")
    dp = lax.axis_index(DP)
    tensor = lax.axis_index(TENSOR)
    bases = [((dp + (1 - 2 * core) * k) * 8 + tensor) * width for k in (0, 1)]
    learn_ids = jnp.stack(bases + [lax.axis_index(Y)])
    target_ids = jnp.stack(bases + [lax.axis_index("x")])

    zeros = jnp.zeros((8, tokens), f32)
    *learn_e, learn_stats, learn = q_values(learn_blocks, learn_heads, learn_ids, zeros.at[0].set(action_all), False, rows)
    *target_e, target_stats = q_values(target_blocks, target_heads, target_ids, zeros, True, rows)

    packed = learn_stats + target_stats
    packed = lax.all_to_all(
        jnp.broadcast_to(packed[None], (64,) + packed.shape), PLANE, 0, 0, tiled=True
    )
    learn_max = jnp.max(packed[:, 0], axis=0)
    target_max = jnp.max(packed[:, 2], axis=0)
    learn_sum = jnp.sum(packed[:, 1] * jnp.exp((packed[:, 0] - learn_max) / temper), axis=0)
    target_sum = jnp.sum(packed[:, 3] * jnp.exp((packed[:, 2] - target_max) / temper), axis=0)
    picked = jnp.sum(packed[:, 4], axis=0)

    target_value = target_max + temper * jnp.log(target_sum)
    offset = jnp.arange(tokens, dtype=jnp.int32) % seq_len
    lengths = jnp.repeat(length_all, seq_len)
    live = (offset < lengths).astype(f32)
    follow = (offset + 1 < lengths).astype(f32)
    shifted = jnp.concatenate([target_value[1:], jnp.zeros((1,), f32)])
    target_y = reward_all + discount * follow * shifted
    delta = live * (picked - target_y)

    vec = jnp.stack(
        [
            action_all,
            kl_weight * live * jnp.exp((learn_stats[0] - learn_max) / temper) / learn_sum,
            kl_weight * live * jnp.exp((target_stats[2] - target_max) / temper) / target_sum,
            delta,
        ]
    )
    vec = jnp.concatenate([vec, jnp.zeros_like(vec)])
    grad_own, grad_sib, partial = gradients(
        learn_e, target_e, learn_heads, learn_ids, vec, rows, feats, traj_total
    )

    partial = lax.all_to_all(partial.reshape(64, rows, feats), PLANE, 0, 0, tiled=True)
    head_grad = head_gradient((grad_own, swap_cores(grad_sib)), (learn, swap_cores(learn)))
    partial, head_grad = lax.optimization_barrier((partial, head_grad))
    hidden_grad = jnp.sum(partial.astype(f32), axis=0).astype(bf16)
    head_grad = head_grad.T

    magnitude = jnp.abs(delta).reshape(8 * trajs, seq_len)
    owner_table = (jnp.arange(16, dtype=jnp.int32)[:, None] == owner_all[None, :]).astype(f32)
    sums = jnp.dot(owner_table, magnitude, precision=lax.Precision.HIGHEST)
    sums = sums + swap_cores(sums)
    priority = lax.dynamic_slice_in_dim(sums, dp, 1, 0)
    return (head_grad, hidden_grad, priority)


def solution(mesh):
    fine = Mesh(mesh.devices.reshape(2, 4, 2, 4, 2), ("yh", "x", "c", "z", "yl"))
    vocab = P(None, DP + TENSOR)
    return jax.shard_map(
        shards,
        mesh=fine,
        in_specs=(P(DP, TENSOR), P(DP, TENSOR), P(DP), vocab, vocab, P(DP), P(DP), P(DP)),
        out_specs=(vocab, P(DP, TENSOR), P(DP, None)),
        check_vma=False,
    )
```

```python
import functools

import jax
import jax.numpy as jnp
from jax import lax
from jax.experimental import pallas as pl
from jax.experimental.pallas import tpu as pltpu
from jax.sharding import Mesh, PartitionSpec as P

temper = 1.0
discount = 0.99
kl_weight = 10.0

DP = ("yh", "x", "c")
TENSOR = ("z", "yl")
PLANE = ("yh", "x", "z", "yl")
Y = ("yh", "yl")


def shift(v, axis, by):
    return lax.ppermute(v, axis, [(i, (i + by) % 4) for i in range(4)])


def swap_cores(v):
    return lax.ppermute(v, "c", [(0, 1), (1, 0)])


def ring_blocks(v, axis):
    ahead, back, across = (shift(v, axis, by) for by in (1, 3, 2))
    return v, ahead, across, back


def gather_ring(v, axis):
    me = lax.axis_index(axis)
    out = jnp.zeros((4,) + v.shape, v.dtype)
    for by, block in enumerate(ring_blocks(v, axis)):
        out = lax.dynamic_update_index_in_dim(out, block, (me - by) & 3, 0)
    return out


VMEM_LIMIT = 60 * 1024 * 1024
NT = (((1,), (1,)), ((), ()))
NN = (((1,), (0,)), ((), ()))


def whole(shape):
    return pl.BlockSpec(shape, lambda j: (0,) * len(shape))


def cost(flops, nbytes, exps=0):
    return pl.CostEstimate(flops=flops, bytes_accessed=nbytes, transcendentals=exps)


def columns_of(ref):
    turned = jnp.concatenate([ref[...]] * 16, axis=0).T
    return [turned[:, k : k + 1] for k in range(8)]


def place_blocks(ids_ref, y_blocks, x_blocks, x_ring, out_ref):
    rows, half = y_blocks[0].shape[-2:]
    feats = 2 * half
    for by, block in enumerate(y_blocks):
        y = (ids_ref[2] - by) & 3
        at = pl.multiple_of((y // 2) * 4 * rows, 4 * rows)
        lane = pl.multiple_of((y % 2) * feats, feats)
        out_ref[pl.ds(at, 4 * rows), pl.ds(lane, half)] = block[...].reshape(4 * rows, half)
    for by, block in enumerate(x_blocks):
        x = (ids_ref[3] - by) & 3 if x_ring else by
        for y in range(4):
            at = pl.multiple_of(((y // 2) * 4 + x) * rows, rows)
            lane = (y % 2) * feats + half
            out_ref[pl.ds(at, rows), lane : lane + half] = block[y]


def q_kernel(learner, ids_ref, vec_ref, *refs):
    blocks, (own_ref, sib_ref, e_own, e_sib, stats_ref, hidden_ref) = refs[:8], refs[8:]
    j = pl.program_id(0)
    place_blocks(ids_ref, blocks[:4], blocks[4:], learner, hidden_ref)
    for head_ref, q_ref in ((own_ref, e_own), (sib_ref, e_sib)):
        part = lax.dot_general(hidden_ref[...], head_ref[...], NT, preferred_element_type=jnp.float32)

        @pl.when(j == 0)
        def _():
            q_ref[...] = part

        @pl.when(j > 0)
        def _():
            q_ref[...] += part

    @pl.when(j == pl.num_programs(0) - 1)
    def _():
        peak = jnp.maximum(
            jnp.max(e_own[...], axis=1, keepdims=True), jnp.max(e_sib[...], axis=1, keepdims=True)
        )
        total = jnp.zeros_like(peak)
        picked = jnp.zeros_like(peak)
        if learner:
            action = columns_of(vec_ref)[0].astype(jnp.int32)
            ids = lax.broadcasted_iota(jnp.int32, e_own.shape, 1)
        for k, q_ref in enumerate((e_own, e_sib)):
            q = q_ref[...]
            if learner:
                hit = ids == action - ids_ref[k]
                picked += jnp.sum(jnp.where(hit, q, 0.0), axis=1, keepdims=True)
            expo = jnp.exp((q - peak) / temper)
            total += jnp.sum(expo, axis=1, keepdims=True)
            q_ref[...] = expo
        lane = lax.broadcasted_iota(jnp.int32, (peak.shape[0], 128), 1)
        first = 0 if learner else 2
        table = jnp.where(lane == first, peak, jnp.where(lane == first + 1, total, 0.0))
        if learner:
            table = jnp.where(lane == 4, picked, table)
        table = table.T[:8]
        if learner:
            stats_ref[...] = table
        else:
            stats_ref[...] = jnp.broadcast_to(table + vec_ref[...], stats_ref.shape)


def q_values(blocks, heads, ids, vec, learner, rows):
    width, feats_all = heads[0].shape
    half = blocks[0].shape[-1]
    feats = 2 * half
    tokens = vec.shape[1]
    block_specs = [pl.BlockSpec((4, rows, half), lambda j: (0, j, 0))] * len(blocks)
    if not learner:
        blocks = blocks[:4] + blocks[4:] * 4
        block_specs = block_specs[:4] + [
            pl.BlockSpec((None, 4, rows, half), lambda j, x=x: (x, 0, j, 0)) for x in range(4)
        ]
    head_spec = pl.BlockSpec((width, 2 * feats), lambda j: (0, j))
    hidden_spec = pl.BlockSpec((tokens, 2 * feats), lambda j: (0, j))
    q_shape = jax.ShapeDtypeStruct((tokens, width), jnp.float32)
    stats_shape = jax.ShapeDtypeStruct((8, tokens) if learner else (64, 8, tokens), jnp.float32)
    hidden_shape = jax.ShapeDtypeStruct((tokens, feats_all), jnp.bfloat16)
    outs = [q_shape, q_shape, stats_shape]
    out_specs = [whole(o.shape) for o in outs]
    scratch = [pltpu.VMEM((tokens, 2 * feats), jnp.bfloat16)]
    if learner:
        outs, out_specs, scratch = outs + [hidden_shape], out_specs + [hidden_spec], []
    return pl.pallas_call(
        functools.partial(q_kernel, learner),
        grid=(feats_all // (2 * feats),),
        in_specs=[pl.BlockSpec(memory_space=pltpu.SMEM), whole(vec.shape)] + block_specs + [head_spec] * 2,
        out_specs=out_specs,
        out_shape=outs,
        scratch_shapes=scratch,
        compiler_params=pltpu.CompilerParams(vmem_limit_bytes=VMEM_LIMIT),
        cost_estimate=cost(
            4 * tokens * width * feats_all, 4 * width * feats_all + 2 * tokens * feats_all, 2 * tokens * width
        ),
    )(ids, vec, *blocks, *heads)


def grad_kernel(
    scale, ids_ref, vec_ref, le_own, le_sib, te_own, te_sib, own_ref, sib_ref,
    turned_own, turned_sib, part_ref, g_own, g_sib,
):
    @pl.when(pl.program_id(0) == 0)
    def _():
        action, learn_gain, target_gain, delta = columns_of(vec_ref)[:4]
        action = action.astype(jnp.int32)
        ids = lax.broadcasted_iota(jnp.int32, le_own.shape, 1)
        for k, (le, te, out, turned) in enumerate(
            ((le_own, te_own, g_own, turned_own), (le_sib, te_sib, g_sib, turned_sib))
        ):
            hit = ids == action - ids_ref[k]
            both = le[...] * learn_gain - te[...] * target_gain
            grad = (jnp.where(hit, delta, 0.0) + both / temper) * scale
            out[...] = grad.astype(jnp.bfloat16)
            turned[...] = grad.T.astype(jnp.bfloat16)

    part = lax.dot_general(g_own[...], own_ref[...], NN, preferred_element_type=jnp.float32)
    part += lax.dot_general(g_sib[...], sib_ref[...], NN, preferred_element_type=jnp.float32)
    part = part.astype(jnp.bfloat16)
    groups, _, rows, feats = part_ref.shape
    for k in range(2):
        part_ref[:, k] = part[:, k * feats : (k + 1) * feats].reshape(groups, rows, feats)


def gradients(learn_e, target_e, heads, ids, vec, rows, feats, traj_total):
    width, feats_all = heads[0].shape
    tokens = vec.shape[1]
    groups = tokens // rows
    head_spec = pl.BlockSpec((width, 2 * feats), lambda j: (0, j))
    g_shape = jax.ShapeDtypeStruct((width, tokens), jnp.bfloat16)
    return pl.pallas_call(
        functools.partial(grad_kernel, 1.0 / traj_total),
        grid=(feats_all // (2 * feats),),
        in_specs=[pl.BlockSpec(memory_space=pltpu.SMEM), whole(vec.shape)]
        + [whole((tokens, width))] * 4
        + [head_spec] * 2,
        out_specs=[whole((width, tokens))] * 2
        + [pl.BlockSpec((groups, 2, rows, feats), lambda j: (0, j, 0, 0))],
        out_shape=[g_shape, g_shape]
        + [jax.ShapeDtypeStruct((groups, feats_all // feats, rows, feats), jnp.bfloat16)],
        scratch_shapes=[pltpu.VMEM((tokens, width), jnp.bfloat16)] * 2,
        compiler_params=pltpu.CompilerParams(vmem_limit_bytes=VMEM_LIMIT),
        cost_estimate=cost(
            4 * tokens * width * feats_all, 4 * width * feats_all + 2 * tokens * feats_all, 0
        ),
    )(ids, vec, *learn_e, *target_e, *heads)


def head_kernel(grad_a, grad_b, hidden_a, hidden_b, out_ref):
    total = lax.dot_general(grad_a[...], hidden_a[...], NN, preferred_element_type=jnp.float32)
    total += lax.dot_general(grad_b[...], hidden_b[...], NN, preferred_element_type=jnp.float32)
    out_ref[...] = total.astype(jnp.bfloat16)


def head_gradient(grads, hiddens):
    width, tokens = grads[0].shape
    feats_all = hiddens[0].shape[1]
    block = feats_all // 4
    return pl.pallas_call(
        head_kernel,
        grid=(4,),
        in_specs=[whole((width, tokens))] * 2 + [pl.BlockSpec((tokens, block), lambda j: (0, j))] * 2,
        out_specs=pl.BlockSpec((width, block), lambda j: (0, j)),
        out_shape=jax.ShapeDtypeStruct((width, feats_all), jnp.bfloat16),
        compiler_params=pltpu.CompilerParams(vmem_limit_bytes=VMEM_LIMIT),
        cost_estimate=cost(4 * tokens * width * feats_all, (2 * width + 4 * tokens) * feats_all),
    )(*grads, *hiddens)


def shards(learn_hidden, target_hidden, reward, learn_head, target_head, action, traj_len, owner):
    f32, bf16 = jnp.float32, jnp.bfloat16
    rows, feats = learn_hidden.shape
    width = learn_head.shape[1]
    trajs = traj_len.shape[0]
    tokens = rows * 8
    seq_len = rows // trajs
    traj_total = trajs * 16

    half = feats // 2

    learn_head, target_head = learn_head.T, target_head.T
    learn_sib = swap_cores(learn_head)

    extra = [action & 255, (action >> 8) & 255, action >> 16, reward, traj_len, owner]
    extra = jnp.concatenate([v.astype(bf16) for v in extra])
    extra = jnp.pad(extra[None], ((0, 15), (0, half - extra.shape[0])))

    both = jnp.stack([learn_hidden, target_hidden]).reshape(2, rows, 2, half).transpose(2, 0, 1, 3)
    both, learn_sib = lax.optimization_barrier((gather_ring(both, "z"), learn_sib))
    block = 4 * rows
    first, second = (
        [both[:, part, head].reshape(block, half) for head in (0, 1)] for part in (0, 1)
    )
    first = gather_ring(jnp.concatenate([first[0], extra, first[1]]), "x")
    second = gather_ring(jnp.concatenate(second), Y)
    first, second = lax.optimization_barrier((first, second))
    learn_y = ring_blocks(first[:, : block + 16], Y)
    learn_x = ring_blocks(second[:, :block], "x")
    first, second = first[:, block + 16 :], second[:, block:]
    first, second, target_head, *near = lax.optimization_barrier(
        (first, second, target_head, learn_y[1], learn_y[3], learn_x[1], learn_x[3])
    )
    target_sib = swap_cores(target_head)
    learn_y = (learn_y[0], near[0], learn_y[2], near[1])
    learn_x = (learn_x[0], near[2], learn_x[2], near[3])
    target_y = ring_blocks(first, Y)
    target_x = lax.all_to_all(
        jnp.broadcast_to(second[None], (4,) + second.shape), "x", 0, 0, tiled=True
    )
    learn_heads, target_heads = (learn_head, learn_sib), (target_head, target_sib)

    mine, other = (learn_y[by][:, block].astype(f32) for by in (0, 2))
    lower = lax.axis_index("yh") == 0
    small = jnp.concatenate([jnp.where(lower, mine, other), jnp.where(lower, other, mine)])

    def field(at, size):
        return small[:, at : at + size].reshape(8 * size)

    action_all = field(0, rows) + 256.0 * field(rows, rows) + 65536.0 * field(2 * rows, rows)
    reward_all = field(3 * rows, rows)
    length_all = field(4 * rows, trajs).astype(jnp.int32)
    owner_all = field(4 * rows + trajs, trajs).astype(jnp.int32)

    core = lax.axis_index("c")
    dp = lax.axis_index(DP)
    tensor = lax.axis_index(TENSOR)
    bases = [((dp + (1 - 2 * core) * k) * 8 + tensor) * width for k in (0, 1)]
    ids = jnp.stack(bases + [lax.axis_index(Y), lax.axis_index("x")])

    vec = jnp.zeros((8, tokens), f32).at[0].set(action_all)
    *learn_e, learn_stats, learn = q_values(
        learn_y + learn_x, learn_heads, ids, vec, True, rows
    )
    *target_e, target_stats = q_values(target_y + (target_x,), target_heads, ids, learn_stats, False, rows)

    packed = lax.all_to_all(target_stats, PLANE, 0, 0, tiled=True)
    learn_max = jnp.max(packed[:, 0], axis=0)
    target_max = jnp.max(packed[:, 2], axis=0)
    learn_sum = jnp.sum(packed[:, 1] * jnp.exp((packed[:, 0] - learn_max) / temper), axis=0)
    target_sum = jnp.sum(packed[:, 3] * jnp.exp((packed[:, 2] - target_max) / temper), axis=0)
    picked = jnp.sum(packed[:, 4], axis=0)

    target_value = target_max + temper * jnp.log(target_sum)
    offset = jnp.arange(tokens, dtype=jnp.int32) % seq_len
    lengths = jnp.repeat(length_all, seq_len)
    live = (offset < lengths).astype(f32)
    follow = (offset + 1 < lengths).astype(f32)
    shifted = jnp.concatenate([target_value[1:], jnp.zeros((1,), f32)])
    target_y = reward_all + discount * follow * shifted
    delta = live * (picked - target_y)

    vec = jnp.stack(
        [
            action_all,
            kl_weight * live * jnp.exp((learn_stats[0] - learn_max) / temper) / learn_sum,
            kl_weight * live * jnp.exp((target_stats[0, 2] - target_max) / temper) / target_sum,
            delta,
        ]
    )
    vec = jnp.concatenate([vec, jnp.zeros_like(vec)])
    grad_own, grad_sib, partial = gradients(
        learn_e, target_e, learn_heads, ids, vec, rows, feats, traj_total
    )

    partial = lax.all_to_all(partial.reshape(64, rows, feats), PLANE, 0, 0, tiled=True)
    head_grad = head_gradient((grad_own, swap_cores(grad_sib)), (learn, swap_cores(learn)))
    partial, head_grad = lax.optimization_barrier((partial, head_grad))
    hidden_grad = jnp.sum(partial.astype(f32), axis=0).astype(bf16)
    head_grad = head_grad.T

    magnitude = jnp.abs(delta).reshape(8 * trajs, seq_len)
    owner_table = (jnp.arange(16, dtype=jnp.int32)[:, None] == owner_all[None, :]).astype(f32)
    sums = jnp.dot(owner_table, magnitude, precision=lax.Precision.HIGHEST)
    sums = sums + swap_cores(sums)
    priority = lax.dynamic_slice_in_dim(sums, dp, 1, 0)
    return (head_grad, hidden_grad, priority)


def solution(mesh):
    fine = Mesh(mesh.devices.reshape(2, 4, 2, 4, 2), ("yh", "x", "c", "z", "yl"))
    vocab = P(None, DP + TENSOR)
    return jax.shard_map(
        shards,
        mesh=fine,
        in_specs=(P(DP, TENSOR), P(DP, TENSOR), P(DP), vocab, vocab, P(DP), P(DP), P(DP)),
        out_specs=(vocab, P(DP, TENSOR), P(DP, None)),
        check_vma=False,
    )
```

```python
import functools

import jax
import jax.numpy as jnp
from jax import lax
from jax.experimental import pallas as pl
from jax.experimental.pallas import tpu as pltpu
from jax.sharding import Mesh, PartitionSpec as P

temper = 1.0
discount = 0.99
kl_weight = 10.0

DP = ("yh", "x", "c")
TENSOR = ("z", "yl")
PLANE = ("yh", "x", "z", "yl")
Y = ("yh", "yl")


def shift(v, axis, by):
    return lax.ppermute(v, axis, [(i, (i + by) % 4) for i in range(4)])


def swap_cores(v):
    return lax.ppermute(v, "c", [(0, 1), (1, 0)])


def ring_blocks(v, axis):
    ahead, back, across = (shift(v, axis, by) for by in (1, 3, 2))
    return v, ahead, across, back


def gather_ring(v, axis):
    me = lax.axis_index(axis)
    out = jnp.zeros((4,) + v.shape, v.dtype)
    for by, block in enumerate(ring_blocks(v, axis)):
        out = lax.dynamic_update_index_in_dim(out, block, (me - by) & 3, 0)
    return out


VMEM_LIMIT = 60 * 1024 * 1024
Q_VMEM_LIMIT = 52 * 1024 * 1024
NT = (((1,), (1,)), ((), ()))
NN = (((1,), (0,)), ((), ()))


def whole(shape):
    return pl.BlockSpec(shape, lambda j: (0,) * len(shape))


def cost(flops, nbytes, exps=0):
    return pl.CostEstimate(flops=flops, bytes_accessed=nbytes, transcendentals=exps)


def columns_of(ref):
    turned = jnp.concatenate([ref[...]] * 16, axis=0).T
    return [turned[:, k : k + 1] for k in range(8)]


def place_blocks(ids_ref, y_blocks, x_blocks, x_ring, out_ref):
    rows, half = y_blocks[0].shape[-2:]
    feats = 2 * half
    for by, block in enumerate(y_blocks):
        y = (ids_ref[2] - by) & 3
        at = pl.multiple_of((y // 2) * 4 * rows, 4 * rows)
        lane = pl.multiple_of((y % 2) * feats, feats)
        out_ref[pl.ds(at, 4 * rows), pl.ds(lane, half)] = block[...].reshape(4 * rows, half)
    for by, block in enumerate(x_blocks):
        x = (ids_ref[3] - by) & 3 if x_ring else by
        for y in range(4):
            at = pl.multiple_of(((y // 2) * 4 + x) * rows, rows)
            lane = (y % 2) * feats + half
            out_ref[pl.ds(at, rows), lane : lane + half] = block[y]


def q_kernel(learner, ids_ref, vec_ref, *refs):
    blocks, (own_ref, sib_ref, e_own, e_sib, stats_ref, hidden_ref) = refs[:8], refs[8:]
    j = pl.program_id(0)
    place_blocks(ids_ref, blocks[:4], blocks[4:], learner, hidden_ref)
    for head_ref, q_ref in ((own_ref, e_own), (sib_ref, e_sib)):
        part = lax.dot_general(hidden_ref[...], head_ref[...], NT, preferred_element_type=jnp.float32)

        @pl.when(j == 0)
        def _():
            q_ref[...] = part

        @pl.when(j > 0)
        def _():
            q_ref[...] += part

    @pl.when(j == pl.num_programs(0) - 1)
    def _():
        peak = jnp.maximum(
            jnp.max(e_own[...], axis=1, keepdims=True), jnp.max(e_sib[...], axis=1, keepdims=True)
        )
        total = jnp.zeros_like(peak)
        picked = jnp.zeros_like(peak)
        if learner:
            action = columns_of(vec_ref)[0].astype(jnp.int32)
            ids = lax.broadcasted_iota(jnp.int32, e_own.shape, 1)
        for k, q_ref in enumerate((e_own, e_sib)):
            q = q_ref[...]
            if learner:
                hit = ids == action - ids_ref[k]
                picked += jnp.sum(jnp.where(hit, q, 0.0), axis=1, keepdims=True)
            expo = jnp.exp((q - peak) / temper)
            total += jnp.sum(expo, axis=1, keepdims=True)
            q_ref[...] = expo
        lane = lax.broadcasted_iota(jnp.int32, (peak.shape[0], 128), 1)
        first = 0 if learner else 2
        table = jnp.where(lane == first, peak, jnp.where(lane == first + 1, total, 0.0))
        if learner:
            table = jnp.where(lane == 4, picked, table)
        table = table.T[:8]
        if learner:
            stats_ref[...] = table
        else:
            stats_ref[...] = jnp.broadcast_to(table + vec_ref[...], stats_ref.shape)


def q_values(blocks, heads, ids, vec, learner, rows):
    width, feats_all = heads[0].shape
    half = blocks[0].shape[-1]
    feats = 2 * half
    tokens = vec.shape[1]
    block_specs = [pl.BlockSpec((4, rows, half), lambda j: (0, j, 0))] * len(blocks)
    if not learner:
        blocks = blocks[:4] + blocks[4:] * 4
        block_specs = block_specs[:4] + [
            pl.BlockSpec((None, 4, rows, half), lambda j, x=x: (x, 0, j, 0)) for x in range(4)
        ]
    head_spec = pl.BlockSpec((width, 2 * feats), lambda j: (0, j))
    hidden_spec = pl.BlockSpec((tokens, 2 * feats), lambda j: (0, j))
    q_shape = jax.ShapeDtypeStruct((tokens, width), jnp.float32)
    stats_shape = jax.ShapeDtypeStruct((8, tokens) if learner else (64, 8, tokens), jnp.float32)
    hidden_shape = jax.ShapeDtypeStruct((tokens, feats_all), jnp.bfloat16)
    outs = [q_shape, q_shape, stats_shape]
    out_specs = [whole(o.shape) for o in outs]
    scratch = [pltpu.VMEM((tokens, 2 * feats), jnp.bfloat16)]
    if learner:
        outs, out_specs, scratch = outs + [hidden_shape], out_specs + [hidden_spec], []
    return pl.pallas_call(
        functools.partial(q_kernel, learner),
        grid=(feats_all // (2 * feats),),
        in_specs=[pl.BlockSpec(memory_space=pltpu.SMEM), whole(vec.shape)] + block_specs + [head_spec] * 2,
        out_specs=out_specs,
        out_shape=outs,
        scratch_shapes=scratch,
        compiler_params=pltpu.CompilerParams(vmem_limit_bytes=Q_VMEM_LIMIT),
        cost_estimate=cost(
            4 * tokens * width * feats_all, 4 * width * feats_all + 2 * tokens * feats_all, 2 * tokens * width
        ),
    )(ids, vec, *blocks, *heads)


def grad_kernel(
    scale, ids_ref, vec_ref, le_own, le_sib, te_own, te_sib, own_ref, sib_ref,
    turned_own, turned_sib, part_ref, g_own, g_sib,
):
    @pl.when(pl.program_id(0) == 0)
    def _():
        action, learn_gain, target_gain, delta = columns_of(vec_ref)[:4]
        action = action.astype(jnp.int32)
        ids = lax.broadcasted_iota(jnp.int32, le_own.shape, 1)
        for k, (le, te, out, turned) in enumerate(
            ((le_own, te_own, g_own, turned_own), (le_sib, te_sib, g_sib, turned_sib))
        ):
            hit = ids == action - ids_ref[k]
            both = le[...] * learn_gain - te[...] * target_gain
            grad = (jnp.where(hit, delta, 0.0) + both / temper) * scale
            out[...] = grad.astype(jnp.bfloat16)
            turned[...] = grad.T.astype(jnp.bfloat16)

    part = lax.dot_general(g_own[...], own_ref[...], NN, preferred_element_type=jnp.float32)
    part += lax.dot_general(g_sib[...], sib_ref[...], NN, preferred_element_type=jnp.float32)
    part = part.astype(jnp.bfloat16)
    groups, _, rows, feats = part_ref.shape
    for k in range(2):
        part_ref[:, k] = part[:, k * feats : (k + 1) * feats].reshape(groups, rows, feats)


def gradients(learn_e, target_e, heads, ids, vec, rows, feats, traj_total):
    width, feats_all = heads[0].shape
    tokens = vec.shape[1]
    groups = tokens // rows
    head_spec = pl.BlockSpec((width, 2 * feats), lambda j: (0, j))
    g_shape = jax.ShapeDtypeStruct((width, tokens), jnp.bfloat16)
    return pl.pallas_call(
        functools.partial(grad_kernel, 1.0 / traj_total),
        grid=(feats_all // (2 * feats),),
        in_specs=[pl.BlockSpec(memory_space=pltpu.SMEM), whole(vec.shape)]
        + [whole((tokens, width))] * 4
        + [head_spec] * 2,
        out_specs=[whole((width, tokens))] * 2
        + [pl.BlockSpec((groups, 2, rows, feats), lambda j: (0, j, 0, 0))],
        out_shape=[g_shape, g_shape]
        + [jax.ShapeDtypeStruct((groups, feats_all // feats, rows, feats), jnp.bfloat16)],
        scratch_shapes=[pltpu.VMEM((tokens, width), jnp.bfloat16)] * 2,
        compiler_params=pltpu.CompilerParams(vmem_limit_bytes=VMEM_LIMIT),
        cost_estimate=cost(
            4 * tokens * width * feats_all, 4 * width * feats_all + 2 * tokens * feats_all, 0
        ),
    )(ids, vec, *learn_e, *target_e, *heads)


def head_kernel(grad_a, grad_b, hidden_a, hidden_b, out_ref):
    total = lax.dot_general(grad_a[...], hidden_a[...], NN, preferred_element_type=jnp.float32)
    total += lax.dot_general(grad_b[...], hidden_b[...], NN, preferred_element_type=jnp.float32)
    out_ref[...] = total.astype(jnp.bfloat16)


def head_gradient(grads, hiddens):
    width, tokens = grads[0].shape
    feats_all = hiddens[0].shape[1]
    block = feats_all // 4
    return pl.pallas_call(
        head_kernel,
        grid=(4,),
        in_specs=[whole((width, tokens))] * 2 + [pl.BlockSpec((tokens, block), lambda j: (0, j))] * 2,
        out_specs=pl.BlockSpec((width, block), lambda j: (0, j)),
        out_shape=jax.ShapeDtypeStruct((width, feats_all), jnp.bfloat16),
        compiler_params=pltpu.CompilerParams(vmem_limit_bytes=VMEM_LIMIT),
        cost_estimate=cost(4 * tokens * width * feats_all, (2 * width + 4 * tokens) * feats_all),
    )(*grads, *hiddens)


def shards(learn_hidden, target_hidden, reward, learn_head, target_head, action, traj_len, owner):
    f32, bf16 = jnp.float32, jnp.bfloat16
    rows, feats = learn_hidden.shape
    width = learn_head.shape[1]
    trajs = traj_len.shape[0]
    tokens = rows * 8
    seq_len = rows // trajs
    traj_total = trajs * 16

    half = feats // 2

    learn_head, target_head = learn_head.T, target_head.T
    learn_sib = swap_cores(learn_head)

    extra = [action & 255, (action >> 8) & 255, action >> 16, reward, traj_len, owner]
    extra = jnp.concatenate([v.astype(bf16) for v in extra])
    extra = jnp.pad(extra[None], ((0, 15), (0, half - extra.shape[0])))

    both = [v[:, at : at + half] for at in (0, half) for v in (learn_hidden, target_hidden)]
    both = jnp.stack(both).reshape(2, 2, rows, half)
    both, learn_sib = lax.optimization_barrier((gather_ring(both, "z"), learn_sib))
    block = 4 * rows
    first, second = (
        [both[:, part, head].reshape(block, half) for head in (0, 1)] for part in (0, 1)
    )
    first = gather_ring(jnp.concatenate([first[0], extra, first[1]]), "x")
    second = gather_ring(jnp.concatenate(second), Y)
    first, second = lax.optimization_barrier((first, second))
    learn_y = ring_blocks(first[:, : block + 16], Y)
    learn_x = ring_blocks(second[:, :block], "x")
    first, second = first[:, block + 16 :], second[:, block:]
    first, second, target_head, *near = lax.optimization_barrier(
        (first, second, target_head, learn_y[1], learn_y[3], learn_x[1], learn_x[3])
    )
    target_sib = swap_cores(target_head)
    learn_y = (learn_y[0], near[0], learn_y[2], near[1])
    learn_x = (learn_x[0], near[2], learn_x[2], near[3])
    target_y = ring_blocks(first, Y)
    target_x = lax.all_to_all(
        jnp.broadcast_to(second[None], (4,) + second.shape), "x", 0, 0, tiled=True
    )
    learn_heads, target_heads = (learn_head, learn_sib), (target_head, target_sib)

    mine, other = (learn_y[by][:, block].astype(f32) for by in (0, 2))
    lower = lax.axis_index("yh") == 0
    small = jnp.concatenate([jnp.where(lower, mine, other), jnp.where(lower, other, mine)])

    def field(at, size):
        return small[:, at : at + size].reshape(8 * size)

    action_all = field(0, rows) + 256.0 * field(rows, rows) + 65536.0 * field(2 * rows, rows)
    reward_all = field(3 * rows, rows)
    length_all = field(4 * rows, trajs).astype(jnp.int32)
    owner_all = field(4 * rows + trajs, trajs).astype(jnp.int32)

    core = lax.axis_index("c")
    dp = lax.axis_index(DP)
    tensor = lax.axis_index(TENSOR)
    bases = [((dp + (1 - 2 * core) * k) * 8 + tensor) * width for k in (0, 1)]
    ids = jnp.stack(bases + [lax.axis_index(Y), lax.axis_index("x")])

    vec = jnp.zeros((8, tokens), f32).at[0].set(action_all)
    *learn_e, learn_stats, learn = q_values(
        learn_y + learn_x, learn_heads, ids, vec, True, rows
    )
    *target_e, target_stats = q_values(target_y + (target_x,), target_heads, ids, learn_stats, False, rows)

    packed = lax.all_to_all(target_stats, PLANE, 0, 0, tiled=True)
    learn_max = jnp.max(packed[:, 0], axis=0)
    target_max = jnp.max(packed[:, 2], axis=0)
    learn_sum = jnp.sum(packed[:, 1] * jnp.exp((packed[:, 0] - learn_max) / temper), axis=0)
    target_sum = jnp.sum(packed[:, 3] * jnp.exp((packed[:, 2] - target_max) / temper), axis=0)
    picked = jnp.sum(packed[:, 4], axis=0)

    target_value = target_max + temper * jnp.log(target_sum)
    offset = jnp.arange(tokens, dtype=jnp.int32) % seq_len
    lengths = jnp.repeat(length_all, seq_len)
    live = (offset < lengths).astype(f32)
    follow = (offset + 1 < lengths).astype(f32)
    shifted = jnp.concatenate([target_value[1:], jnp.zeros((1,), f32)])
    target_y = reward_all + discount * follow * shifted
    delta = live * (picked - target_y)

    vec = jnp.stack(
        [
            action_all,
            kl_weight * live * jnp.exp((learn_stats[0] - learn_max) / temper) / learn_sum,
            kl_weight * live * jnp.exp((target_stats[0, 2] - target_max) / temper) / target_sum,
            delta,
        ]
    )
    vec = jnp.concatenate([vec, jnp.zeros_like(vec)])
    grad_own, grad_sib, partial = gradients(
        learn_e, target_e, learn_heads, ids, vec, rows, feats, traj_total
    )

    partial = lax.all_to_all(partial.reshape(64, rows, feats), PLANE, 0, 0, tiled=True)
    head_grad = head_gradient((grad_own, swap_cores(grad_sib)), (learn, swap_cores(learn)))
    partial, head_grad = lax.optimization_barrier((partial, head_grad))
    hidden_grad = jnp.sum(partial.astype(f32), axis=0).astype(bf16)
    head_grad = head_grad.T

    magnitude = jnp.abs(delta).reshape(8 * trajs, seq_len)
    owner_table = (jnp.arange(16, dtype=jnp.int32)[:, None] == owner_all[None, :]).astype(f32)
    sums = jnp.dot(owner_table, magnitude, precision=lax.Precision.HIGHEST)
    sums = sums + swap_cores(sums)
    priority = lax.dynamic_slice_in_dim(sums, dp, 1, 0)
    return (head_grad, hidden_grad, priority)


def solution(mesh):
    fine = Mesh(mesh.devices.reshape(2, 4, 2, 4, 2), ("yh", "x", "c", "z", "yl"))
    vocab = P(None, DP + TENSOR)
    return jax.shard_map(
        shards,
        mesh=fine,
        in_specs=(P(DP, TENSOR), P(DP, TENSOR), P(DP), vocab, vocab, P(DP), P(DP), P(DP)),
        out_specs=(vocab, P(DP, TENSOR), P(DP, None)),
        check_vma=False,
    )
```
